256 devices in a mesh: box: 32 (over y, x, z_hi), coef: 8 (over z_lo, core).
Axes of the slice: x: 4, y: 4, z: 8 (z_hi: 2, z_lo: 4; z = z_hi * 4 + z_lo), core: 2. Of those that a mesh axis runs over, the one named last changes fastest.
Arguments:
- coefficients: bfloat16 [32, 24576, 512], P('box', 'coef'), may hold values from -6 to 6
- interp: bfloat16 [4, 2, 2, 2, 256, 256], replicated, may hold values from -0.1875 to 0.1875
- switch: bfloat16 [32, 2, 256, 256], P('box', None, 'coef'), may hold values from -0.25 to 0.25
- grid_offsets: int32 [32, 24576, 2], P('box', 'coef'), may hold values from 0 to 63
Outputs:
- switched: float32 [32, 24576, 512], P('box', 'coef')
The draws below stay inside these ranges and needn't reach their ends.
All inputs are finite; a program needn't handle non-finite values.
Results may differ from the reference program's by a relative error of at most 0.0063.
Values may be sent and summed in bfloat16 or wider, within the bound.
A program may use at most 128 MiB of HBM per device.

```python
import math
import jax
import jax.numpy as jnp
from jax import lax

SIDE = 16
R = 256
LEVELS = 4
Q = 24576
NB = 32


def place_ends(entries, key, smallest, top_value):
    extent = entries.shape
    place = [jax.random.randint(jax.random.fold_in(key, axis), (), 0, extent[axis]) for axis in range(len(extent))]
    entries = entries.at[tuple(place)].set(smallest)
    longest = extent.index(max(extent))
    place[longest] = (place[longest] + 1) % extent[longest]
    return entries.at[tuple(place)].set(top_value)


def level_of(rng, extent, split, least, top_value):
    loudness, own = 1.0, jax.random.fold_in(rng, 6)
    for axis_at, blocks in split:
        draws = jnp.exp(jax.random.uniform(jax.random.fold_in(own, axis_at), (blocks,), jnp.float32, least / len(split), top_value / len(split)))
        loudness = loudness * jnp.repeat(draws, extent[axis_at] // blocks).reshape([-1 if axis == axis_at else 1 for axis in range(len(extent))])
    return loudness


def gaussian(stream_key, dims, spread, limit, split=(), held_as=jnp.bfloat16):
    values = spread * jax.random.normal(stream_key, dims, jnp.float32)
    if split:
        values = values * level_of(stream_key, dims, split, -0.22, 0.18)
    return jnp.clip(values, -limit, limit).astype(held_as)


def setup_inputs(seed: int = 0) -> dict:
    key_of = jax.random.split(jax.random.key(seed), 5)
    return {
        "coefficients": gaussian(key_of[0], (NB, Q, 2 * R), 1.0, 6.0, ((0, 32), (1, 8))),
        "interp": gaussian(key_of[1], (LEVELS, 2, 2, 2, R, R), (4 * R) ** -0.5, 0.1875),
        "switch": gaussian(key_of[2], (NB, 2, R, R), (2 * R) ** -0.5, 0.25, ((0, 32), (2, 8))),
        "grid_offsets": place_ends(jax.random.randint(key_of[3], (NB, Q, 2), 0, 64), jax.random.fold_in(key_of[3], 1), 0, 63).astype(jnp.int32),
    }


def block(real_part, imag_part):
    top = jnp.concatenate([real_part, imag_part], axis=1)
    bottom = jnp.concatenate([-imag_part, real_part], axis=1)
    return jnp.concatenate([top, bottom], axis=0)


def rotate(state, offsets, level):
    points = jnp.arange(R, dtype=jnp.int32)
    point_x = points // SIDE
    point_y = points % SIDE
    phase = ((level + 1) * (offsets[..., 0:1] * point_x + offsets[..., 1:2] * point_y)) % 64
    angle = phase.astype(jnp.float32) * (2.0 * math.pi / 64.0)
    cosine = jnp.cos(angle)
    sine = jnp.sin(angle)
    real_in = state[..., :R]
    imag_in = state[..., R:]
    return jnp.concatenate([real_in * cosine - imag_in * sine, real_in * sine + imag_in * cosine], axis=-1)


def reference(coefficients, interp, switch, grid_offsets):
    state = coefficients.astype(jnp.float32)
    boxes = jnp.arange(NB, dtype=jnp.int32)
    for level in range(LEVELS):
        rotated = rotate(state, grid_offsets, level).astype(jnp.bfloat16)
        partner = rotated[boxes ^ (1 << level)]
        matrices = interp[level]

        def one_box(index):
            bit = (index >> level) & 1
            own = block(matrices[bit, bit, 0], matrices[bit, bit, 1])
            cross = block(matrices[bit, 1 - bit, 0], matrices[bit, 1 - bit, 1])
            first = jnp.dot(rotated[index], own, preferred_element_type=jnp.float32)
            second = jnp.dot(partner[index], cross, preferred_element_type=jnp.float32)
            return first + second

        state = lax.map(one_box, boxes)
    leaving = state.astype(jnp.bfloat16)

    def switch_box(index):
        matrix = block(switch[index, 0], switch[index, 1])
        return jnp.dot(leaving[index], matrix, preferred_element_type=jnp.float32)

    return lax.map(switch_box, boxes)
```

```python
import math

import jax
import jax.numpy as jnp
from jax import lax
from jax.experimental import pallas as pl
from jax.experimental.pallas import tpu as pltpu
from jax.sharding import PartitionSpec as P

SIDE = 16
MEMBERS = 16
CHUNK = 32
WINDOW = 256
MESH = pl.DeviceIdType.MESH


def turn(phase):
    share = phase * (1.0 / 64.0)
    share = share - jnp.floor(share + 0.5)
    half = share * math.pi
    square = half * half
    sine = half * (1.0 + square * (-1.0 / 6 + square * (1.0 / 120 + square * (-1.0 / 5040 + square * (
        1.0 / 362880 + square * (-1.0 / 39916800 + square * (1.0 / 6227020800)))))))
    cosine = 1.0 + square * (-0.5 + square * (1.0 / 24 + square * (-1.0 / 720 + square * (
        1.0 / 40320 + square * (-1.0 / 3628800 + square * (1.0 / 479001600))))))
    return 1.0 - 2.0 * sine * sine, 2.0 * sine * cosine


def boxes_with(bit, level):
    return [b for b in range(MEMBERS) if b >> level & 1 == bit]


def middle(
    coef_ref, interp_ref, switch_ref, offsets_ref, home_ref, whole_ref,
    arrived, leaving, weights, windows, columns, cosines, sines, cosine_now, sine_now, rotated,
    in_send, in_recv, out_send, out_recv, off_send, off_recv, sw_send, sw_recv, weight_sem,
):
    box, coef = lax.axis_index("box"), lax.axis_index("coef")
    me, base = box % MEMBERS, box // MEMBERS * MEMBERS
    share = coef_ref.shape[1]
    rank = interp_ref.shape[-1]
    levels = interp_ref.shape[0]
    chunks = share // CHUNK
    parts = lax.axis_size("coef")
    rows = switch_ref.shape[1]

    def member(step):
        return (me + step) % MEMBERS

    barrier = pltpu.get_barrier_semaphore()
    for step in range(1, MEMBERS):
        pl.semaphore_signal(barrier, inc=1, device_id=(base + member(step), coef), device_id_type=MESH)
    for step in range(1, parts):
        pl.semaphore_signal(barrier, inc=1, device_id=(box, (coef + step) % parts), device_id_type=MESH)
    pl.semaphore_wait(barrier, MEMBERS - 1 + parts - 1)

    def window(j):
        return offsets_ref.at[:, pl.ds(pl.multiple_of(128 * (3 * (j // 2) + j % 2), 128), WINDOW)]

    def send(src, dst, send_sem, recv_sem, j):
        return pltpu.make_async_remote_copy(
            src, dst, send_sem, recv_sem, device_id=(base + j, coef), device_id_type=MESH
        )

    for step in range(1, MEMBERS):
        j = member(step)
        send(window(j), windows.at[me], off_send, off_recv, j).start()
    pltpu.make_async_copy(window(me), windows.at[me], off_recv).start()

    def at(c):
        return pl.ds(pl.multiple_of(c * CHUNK, CHUNK), CHUNK)

    def send_in(c, carry):
        for step in range(1, MEMBERS):
            j = member(step)
            send(coef_ref.at[j, at(c)], arrived.at[me, at(c)], in_send, in_recv.at[c], j).start()
        pltpu.make_async_copy(coef_ref.at[me, at(c)], arrived.at[me, at(c)], in_recv.at[c]).start()
        return carry

    lax.fori_loop(0, chunks, send_in, 0)

    def piece(src, owner, step):
        return pltpu.make_async_remote_copy(
            src, whole_ref.at[:, pl.ds(pl.multiple_of(owner * rows, rows), rows)], sw_send, sw_recv,
            device_id=(box, (coef + step) % parts), device_id_type=MESH,
        )

    for step in range(1, parts):
        piece(switch_ref, coef, step).start()
    pltpu.make_async_copy(
        switch_ref, whole_ref.at[:, pl.ds(pl.multiple_of(coef * rows, rows), rows)], sw_recv
    ).start()

    loads = []
    for level in range(levels):
        for bit in range(2):
            for side in range(2):
                pair = interp_ref.at[level, bit, bit if side == 0 else 1 - bit]
                top = 2 * rank * side
                for part, row, column in ((0, 0, 0), (1, 0, rank), (0, rank, rank)):
                    loads.append(pltpu.make_async_copy(
                        pair.at[part],
                        weights.at[level, bit, pl.ds(top + row, rank), pl.ds(column, rank)],
                        weight_sem.at[len(loads)],
                    ))
    for load in loads:
        load.start()
    for load in loads:
        load.wait()

    def negate(i, carry):
        level, bit, side = i // 4, i // 2 % 2, i % 2
        top = 2 * rank * side
        weights[level, bit, pl.ds(pl.multiple_of(top + rank, rank), rank), :rank] = -weights[
            level, bit, pl.ds(pl.multiple_of(top, rank), rank), rank:
        ]
        return carry

    lax.fori_loop(0, 4 * levels, negate, 0)

    pltpu.make_async_copy(windows, windows, off_recv).wait()
    columns[...] = jnp.transpose(
        windows[...].reshape(2 * MEMBERS, WINDOW).astype(jnp.float32), (1, 0)
    )
    points = lax.broadcasted_iota(jnp.int32, (1, rank), 1)
    point_x = (points // SIDE).astype(jnp.float32)
    point_y = (points % SIDE).astype(jnp.float32)
    skip = 64 * (me % 2)

    def compute(c, carry):
        pair = columns[pl.ds(pl.multiple_of(skip + c * CHUNK, CHUNK), CHUNK), :]
        for b in range(MEMBERS):
            phase = pair[:, 2 * b:2 * b + 1] * point_x + pair[:, 2 * b + 1:2 * b + 2] * point_y
            cosine, sine = turn(phase)
            cosines[b] = cosine
            sines[b] = sine

        pltpu.make_async_copy(arrived.at[:, at(c)], arrived.at[:, at(c)], in_recv.at[c]).wait()

        for b in range(MEMBERS):
            state = arrived[b, at(c), :].astype(jnp.float32)
            real, imag = state[:, :rank], state[:, rank:]
            cosine, sine = cosines[b], sines[b]
            rotated[0, b, :, :rank] = (real * cosine - imag * sine).astype(jnp.bfloat16)
            rotated[0, b, :, rank:] = (real * sine + imag * cosine).astype(jnp.bfloat16)

        for level in range(levels):
            now, later = level % 2, 1 - level % 2
            for bit in range(2):
                own = jnp.concatenate([rotated[now, b] for b in boxes_with(bit, level)], axis=0)
                cross = jnp.concatenate(
                    [rotated[now, b ^ 1 << level] for b in boxes_with(bit, level)], axis=0
                )
                state = jnp.dot(
                    jnp.concatenate([own, cross], axis=1), weights[level, bit],
                    preferred_element_type=jnp.float32,
                )
                for k, b in enumerate(boxes_with(bit, level)):
                    mine = state[k * CHUNK:(k + 1) * CHUNK]
                    if level == levels - 1:
                        leaving[b, at(c), :] = mine.astype(jnp.bfloat16)
                        continue
                    cosine, sine = cosines[b], sines[b]
                    before_c = cosine if level == 0 else cosine_now[b]
                    before_s = sine if level == 0 else sine_now[b]
                    next_c = before_c * cosine - before_s * sine
                    next_s = before_c * sine + before_s * cosine
                    if level < levels - 2:
                        cosine_now[b] = next_c
                        sine_now[b] = next_s
                    real, imag = mine[:, :rank], mine[:, rank:]
                    rotated[later, b, :, :rank] = (real * next_c - imag * next_s).astype(jnp.bfloat16)
                    rotated[later, b, :, rank:] = (real * next_s + imag * next_c).astype(jnp.bfloat16)

        for step in range(1, MEMBERS):
            j = member(step)
            send(leaving.at[j, at(c)], home_ref.at[me, at(c)], out_send, out_recv, j).start()
        pltpu.make_async_copy(leaving.at[me, at(c)], home_ref.at[me, at(c)], out_recv).start()
        return carry

    lax.fori_loop(0, chunks, compute, 0)

    others = pl.ds(0, MEMBERS - 1)
    send(coef_ref.at[others], arrived.at[others], in_send, out_recv, member(1)).wait_send()
    send(leaving.at[others], home_ref.at[others], out_send, out_recv, member(1)).wait_send()
    send(windows.at[others], windows.at[others], off_send, out_recv, member(1)).wait_send()
    sent = whole_ref.at[:, pl.ds(0, rows * (parts - 1))]
    send(sent, sent, sw_send, out_recv, member(1)).wait_send()
    pltpu.make_async_copy(whole_ref, whole_ref, sw_recv).wait()
    pltpu.make_async_copy(home_ref, home_ref, out_recv).wait()


def last(leaving_ref, switch_ref, out_ref, matrix):
    rank = switch_ref.shape[-1]

    @pl.when(pl.program_id(0) == 0)
    def _():
        matrix[:rank, :rank] = switch_ref[0]
        matrix[:rank, rank:] = switch_ref[1]
        matrix[rank:, :rank] = -switch_ref[1]
        matrix[rank:, rank:] = switch_ref[0]

    out_ref[...] = jnp.dot(leaving_ref[...], matrix[...], preferred_element_type=jnp.float32)


def body(coefficients, interp, switch, grid_offsets):
    _, rows, width = coefficients.shape
    rank = interp.shape[-1]
    levels = interp.shape[0]
    share = rows // MEMBERS
    chunks = share // CHUNK
    bf16, f32 = jnp.bfloat16, jnp.float32
    anywhere = pl.BlockSpec(memory_space=pl.ANY)
    dma = pltpu.SemaphoreType.DMA
    home, whole = pl.pallas_call(
        middle,
        out_shape=(
            jax.ShapeDtypeStruct((MEMBERS, share, width), bf16),
            jax.ShapeDtypeStruct((2, rank, rank), bf16),
        ),
        in_specs=[anywhere] * 4,
        out_specs=(anywhere, anywhere),
        scratch_shapes=[
            pltpu.VMEM((MEMBERS, share, width), bf16),
            pltpu.VMEM((MEMBERS, share, width), bf16),
            pltpu.VMEM((levels, 2, 2 * width, width), bf16),
            pltpu.VMEM((MEMBERS, 2, WINDOW), jnp.int32),
            pltpu.VMEM((WINDOW, 2 * MEMBERS), f32),
            pltpu.VMEM((MEMBERS, CHUNK, rank), f32),
            pltpu.VMEM((MEMBERS, CHUNK, rank), f32),
            pltpu.VMEM((MEMBERS, CHUNK, rank), f32),
            pltpu.VMEM((MEMBERS, CHUNK, rank), f32),
            pltpu.VMEM((2, MEMBERS, CHUNK, width), bf16),
            dma, dma((chunks,)), dma, dma, dma, dma, dma, dma, dma((12 * levels,)),
        ],
        compiler_params=pltpu.CompilerParams(
            collective_id=0, has_side_effects=True, vmem_limit_bytes=48 << 20
        ),
        name="middle",
    )(coefficients.reshape(MEMBERS, share, width), interp, switch[0], jnp.swapaxes(grid_offsets[0], 0, 1))
    tile = 512
    switched = pl.pallas_call(
        last,
        grid=(rows // tile,),
        out_shape=jax.ShapeDtypeStruct((rows, width), f32),
        in_specs=[
            pl.BlockSpec((tile, width), lambda i: (i, 0)),
            pl.BlockSpec((2, rank, rank), lambda i: (0, 0, 0)),
        ],
        out_specs=pl.BlockSpec((tile, width), lambda i: (i, 0)),
        scratch_shapes=[pltpu.VMEM((width, width), bf16)],
        compiler_params=pltpu.CompilerParams(vmem_limit_bytes=32 << 20),
        name="last",
    )(home.reshape(rows, width), whole)
    return switched[None]


def solution(mesh):
    in_specs = (P("box", "coef", None), P(), P("box", None, "coef", None), P("box", "coef", None))
    out_specs = P("box", "coef", None)
    return jax.shard_map(body, mesh=mesh, in_specs=in_specs, out_specs=out_specs, check_vma=False)
```

```python
import math

import jax
import jax.numpy as jnp
from jax import lax
from jax.experimental import pallas as pl
from jax.experimental.pallas import tpu as pltpu
from jax.sharding import PartitionSpec as P

SIDE = 16
MEMBERS = 16
CHUNK = 64
WINDOW = 256
MESH = pl.DeviceIdType.MESH
STEPS = [(0, 0, 0)] + [
    (y, x, z) for x, y in ((0, 0), (1, 0), (2, 0), (3, 0), (0, 1), (1, 1), (2, 1), (3, 1)) for z in (1, 0) if x + y + z
]


def turn(phase):
    share = phase * (1.0 / 64.0)
    share = share - jnp.floor(share + 0.5)
    half = share * math.pi
    square = half * half
    sine = half * (1.0 + square * (-1.0 / 6 + square * (1.0 / 120 + square * (-1.0 / 5040 + square * (
        1.0 / 362880 + square * (-1.0 / 39916800 + square * (1.0 / 6227020800)))))))
    cosine = 1.0 + square * (-0.5 + square * (1.0 / 24 + square * (-1.0 / 720 + square * (
        1.0 / 40320 + square * (-1.0 / 3628800 + square * (1.0 / 479001600))))))
    return 1.0 - 2.0 * sine * sine, 2.0 * sine * cosine


def boxes_with(bit, level):
    return [b for b in range(MEMBERS) if b >> level & 1 == bit]


def middle(
    coef_ref, interp_ref, switch_ref, offsets_ref, out_ref,
    arrived, leaving, home, weights, whole, matrix, windows, columns,
    cosines, sines, cosine_now, sine_now, rotated,
    in_send, in_recv, out_send, out_recv, off_send, off_recv, sw_send, sw_recv, sw_other, weight_sem,
):
    box, coef = lax.axis_index("box"), lax.axis_index("coef")
    me, base = box % MEMBERS, box // MEMBERS * MEMBERS
    me_y, me_x, me_z = me // 8, me // 2 % 4, me % 2
    share = coef_ref.shape[1]
    rank = interp_ref.shape[-1]
    levels = interp_ref.shape[0]
    chunks = share // CHUNK
    parts = lax.axis_size("coef")
    rows = switch_ref.shape[1]

    def member(step):
        y, x, z = STEPS[step]
        return (me_y + y) % 2 * 8 + (me_x + x) % 4 * 2 + (me_z + z) % 2

    barrier = pltpu.get_barrier_semaphore()
    for step in range(1, MEMBERS):
        pl.semaphore_signal(barrier, inc=1, device_id=(base + member(step), coef), device_id_type=MESH)
    other_core = coef + 1 - 2 * (coef % 2)
    pl.semaphore_signal(barrier, inc=1, device_id=(box, other_core), device_id_type=MESH)
    for step in range(2, parts, 2):
        pl.semaphore_signal(barrier, inc=1, device_id=(box, (coef + step) % parts), device_id_type=MESH)
    pl.semaphore_wait(barrier, MEMBERS - 1 + parts // 2)

    def window(j):
        return offsets_ref.at[:, pl.ds(pl.multiple_of(128 * (3 * (j // 2) + j % 2), 128), WINDOW)]

    def send(src, dst, send_sem, recv_sem, j):
        return pltpu.make_async_remote_copy(
            src, dst, send_sem, recv_sem, device_id=(base + j, coef), device_id_type=MESH
        )

    def at(c):
        return pl.ds(pl.multiple_of(c * CHUNK, CHUNK), CHUNK)

    def rows_of(owner):
        return whole.at[:, pl.ds(pl.multiple_of(owner * rows, rows), rows)]

    def piece(src, owner, recv_sem, target):
        return pltpu.make_async_remote_copy(
            src, rows_of(owner), sw_send, recv_sem, device_id=(box, target), device_id_type=MESH
        )

    for step in range(2, parts, 2):
        piece(switch_ref, coef, sw_recv, (coef + step) % parts).start()
    pltpu.make_async_copy(switch_ref, rows_of(coef), sw_recv).start()

    def send_in(c, carry):
        for step in range(1, MEMBERS):
            j = member(step)
            send(coef_ref.at[j, at(c)], arrived.at[me, at(c)], in_send, in_recv.at[c], j).start()
        pltpu.make_async_copy(coef_ref.at[me, at(c)], arrived.at[me, at(c)], in_recv.at[c]).start()
        return carry

    send_in(0, 0)
    for step in range(1, MEMBERS):
        j = member(step)
        send(window(j), windows.at[me], off_send, off_recv, j).start()
    pltpu.make_async_copy(window(me), windows.at[me], off_recv).start()
    lax.fori_loop(1, chunks, send_in, 0)

    loads = []
    for level in range(levels):
        for bit in range(2):
            for side in range(2):
                pair = interp_ref.at[level, bit, bit if side == 0 else 1 - bit]
                top = 2 * rank * side
                for part, row, column in ((0, 0, 0), (1, 0, rank), (0, rank, rank)):
                    loads.append(pltpu.make_async_copy(
                        pair.at[part],
                        weights.at[level, bit, pl.ds(top + row, rank), pl.ds(column, rank)],
                        weight_sem.at[len(loads)],
                    ))
    for load in loads:
        load.start()
    for load in loads:
        load.wait()

    def negate(i, carry):
        level, bit, side = i // 4, i // 2 % 2, i % 2
        top = 2 * rank * side
        weights[level, bit, pl.ds(pl.multiple_of(top + rank, rank), rank), :rank] = -weights[
            level, bit, pl.ds(pl.multiple_of(top, rank), rank), rank:
        ]
        return carry

    lax.fori_loop(0, 4 * levels, negate, 0)

    pltpu.make_async_copy(windows, windows, off_recv).wait()
    columns[...] = jnp.transpose(
        windows[...].reshape(2 * MEMBERS, WINDOW).astype(jnp.float32), (1, 0)
    )
    points = lax.broadcasted_iota(jnp.int32, (1, rank), 1)
    point_x = (points // SIDE).astype(jnp.float32)
    point_y = (points % SIDE).astype(jnp.float32)
    skip = 64 * (me % 2)

    def compute(c, carry):
        pair = columns[pl.ds(pl.multiple_of(skip + c * CHUNK, CHUNK), CHUNK), :]
        for b in range(MEMBERS):
            phase = pair[:, 2 * b:2 * b + 1] * point_x + pair[:, 2 * b + 1:2 * b + 2] * point_y
            cosine, sine = turn(phase)
            cosines[b] = cosine
            sines[b] = sine

        pltpu.make_async_copy(arrived.at[:, at(c)], arrived.at[:, at(c)], in_recv.at[c]).wait()

        for b in range(MEMBERS):
            state = arrived[b, at(c), :].astype(jnp.float32)
            real, imag = state[:, :rank], state[:, rank:]
            cosine, sine = cosines[b], sines[b]
            rotated[0, b, :, :rank] = (real * cosine - imag * sine).astype(jnp.bfloat16)
            rotated[0, b, :, rank:] = (real * sine + imag * cosine).astype(jnp.bfloat16)

        for level in range(levels):
            now, later = level % 2, 1 - level % 2
            for bit in range(2):
                own = jnp.concatenate([rotated[now, b] for b in boxes_with(bit, level)], axis=0)
                cross = jnp.concatenate(
                    [rotated[now, b ^ 1 << level] for b in boxes_with(bit, level)], axis=0
                )
                state = jnp.dot(
                    jnp.concatenate([own, cross], axis=1), weights[level, bit],
                    preferred_element_type=jnp.float32,
                )
                for k, b in enumerate(boxes_with(bit, level)):
                    mine = state[k * CHUNK:(k + 1) * CHUNK]
                    if level == levels - 1:
                        leaving[b, at(c), :] = mine.astype(jnp.bfloat16)
                        continue
                    cosine, sine = cosines[b], sines[b]
                    before_c = cosine if level == 0 else cosine_now[b]
                    before_s = sine if level == 0 else sine_now[b]
                    next_c = before_c * cosine - before_s * sine
                    next_s = before_c * sine + before_s * cosine
                    if level < levels - 2:
                        cosine_now[b] = next_c
                        sine_now[b] = next_s
                    real, imag = mine[:, :rank], mine[:, rank:]
                    rotated[later, b, :, :rank] = (real * next_c - imag * next_s).astype(jnp.bfloat16)
                    rotated[later, b, :, rank:] = (real * next_s + imag * next_c).astype(jnp.bfloat16)

        for step in range(1, MEMBERS):
            j = member(step)
            send(leaving.at[j, at(c)], home.at[me, at(c)], out_send, out_recv.at[c], j).start()
        pltpu.make_async_copy(leaving.at[me, at(c)], home.at[me, at(c)], out_recv.at[c]).start()
        return carry

    lax.fori_loop(0, chunks, compute, 0)

    half = whole.at[:, pl.ds(0, rows * (parts // 2))]
    pltpu.make_async_copy(half, half, sw_recv).wait()
    for step in range(0, parts, 2):
        owner = (coef + step) % parts
        piece(rows_of(owner), owner, sw_other, other_core).start()
    pltpu.make_async_copy(half, half, sw_other).wait()
    matrix[:rank, :rank] = whole[0]
    matrix[:rank, rank:] = whole[1]
    matrix[rank:, :rank] = -whole[1]
    matrix[rank:, rank:] = whole[0]

    def finish(c, carry):
        pltpu.make_async_copy(home.at[:, at(c)], home.at[:, at(c)], out_recv.at[c]).wait()
        state = home[:, at(c), :].reshape(MEMBERS * CHUNK, 2 * rank)
        switched = jnp.dot(state, matrix[...], preferred_element_type=jnp.float32)
        out_ref[:, at(c), :] = switched.reshape(MEMBERS, CHUNK, 2 * rank)
        return carry

    lax.fori_loop(0, chunks, finish, 0)

    others = pl.ds(0, MEMBERS - 1)
    send(coef_ref.at[others], arrived.at[others], in_send, off_recv, member(1)).wait_send()
    send(leaving.at[others], home.at[others], out_send, off_recv, member(1)).wait_send()
    send(windows.at[others], windows.at[others], off_send, off_recv, member(1)).wait_send()
    sent = whole.at[:, pl.ds(0, rows * (parts - 1))]
    send(sent, sent, sw_send, off_recv, member(1)).wait_send()


def body(coefficients, interp, switch, grid_offsets):
    _, rows, width = coefficients.shape
    rank = interp.shape[-1]
    levels = interp.shape[0]
    share = rows // MEMBERS
    chunks = share // CHUNK
    bf16, f32 = jnp.bfloat16, jnp.float32
    dma = pltpu.SemaphoreType.DMA
    operands = (
        coefficients.reshape(MEMBERS, share, width), interp, switch[0], jnp.swapaxes(grid_offsets[0], 0, 1)
    )
    switched = pl.pallas_call(
        middle,
        out_shape=pltpu.VMEM((MEMBERS, share, width), f32),
        in_specs=[pl.BlockSpec(memory_space=pl.ANY)] * 4,
        out_specs=pl.BlockSpec(memory_space=pltpu.VMEM),
        scratch_shapes=[
            pltpu.VMEM((MEMBERS, share, width), bf16),
            pltpu.VMEM((MEMBERS, share, width), bf16),
            pltpu.VMEM((MEMBERS, share, width), bf16),
            pltpu.VMEM((levels, 2, 2 * width, width), bf16),
            pltpu.VMEM((2, rank, rank), bf16),
            pltpu.VMEM((width, width), bf16),
            pltpu.VMEM((MEMBERS, 2, WINDOW), jnp.int32),
            pltpu.VMEM((WINDOW, 2 * MEMBERS), f32),
            pltpu.VMEM((MEMBERS, CHUNK, rank), f32),
            pltpu.VMEM((MEMBERS, CHUNK, rank), f32),
            pltpu.VMEM((MEMBERS, CHUNK, rank), f32),
            pltpu.VMEM((MEMBERS, CHUNK, rank), f32),
            pltpu.VMEM((2, MEMBERS, CHUNK, width), bf16),
            dma, dma((chunks,)), dma, dma((chunks,)), dma, dma, dma, dma, dma, dma((12 * levels,)),
        ],
        compiler_params=pltpu.CompilerParams(
            collective_id=0, has_side_effects=True, vmem_limit_bytes=48 << 20
        ),
        name="middle",
    )(*[pltpu.with_memory_space_constraint(operand, pltpu.HBM) for operand in operands])
    return switched.reshape(1, rows, width)


def solution(mesh):
    in_specs = (P("box", "coef", None), P(), P("box", None, "coef", None), P("box", "coef", None))
    out_specs = P("box", "coef", None)
    return jax.shard_map(body, mesh=mesh, in_specs=in_specs, out_specs=out_specs, check_vma=False)
```

```python
import math

import jax
import jax.numpy as jnp
from jax import lax
from jax.experimental import pallas as pl
from jax.experimental.pallas import tpu as pltpu
from jax.sharding import PartitionSpec as P

SIDE = 16
MEMBERS = 16
CHUNK = 96
PIECE = 4
WINDOW = 256
MESH = pl.DeviceIdType.MESH
STEPS = [(0, 0, 0)] + [
    (y, x, z) for x, y in ((0, 0), (1, 0), (2, 0), (3, 0), (0, 1), (1, 1), (2, 1), (3, 1)) for z in (1, 0) if x + y + z
]


def turn(phase):
    share = phase * (1.0 / 64.0)
    share = share - jnp.floor(share + 0.5)
    half = share * math.pi
    square = half * half
    sine = half * (1.0 + square * (-1.0 / 6 + square * (1.0 / 120 + square * (-1.0 / 5040 + square * (
        1.0 / 362880 + square * (-1.0 / 39916800 + square * (1.0 / 6227020800)))))))
    cosine = 1.0 + square * (-0.5 + square * (1.0 / 24 + square * (-1.0 / 720 + square * (
        1.0 / 40320 + square * (-1.0 / 3628800 + square * (1.0 / 479001600))))))
    return 1.0 - 2.0 * sine * sine, 2.0 * sine * cosine


def boxes_with(bit, level):
    return [b for b in range(MEMBERS) if b >> level & 1 == bit]


def middle(
    coef_ref, interp_ref, switch_ref, offsets_ref, early_ref, home, matrix,
    arrived, leaving, weights, whole, windows, columns,
    cosines, sines, cosine_now, sine_now, rotated,
    in_send, in_recv, out_send, out_recv, off_send, off_recv, sw_send, sw_recv, sw_other, weight_sem,
):
    box, coef = lax.axis_index("box"), lax.axis_index("coef")
    me, base = box % MEMBERS, box // MEMBERS * MEMBERS
    me_y, me_x, me_z = me // 8, me // 2 % 4, me % 2
    share = coef_ref.shape[1]
    rank = interp_ref.shape[-1]
    levels = interp_ref.shape[0]
    chunks = share // CHUNK
    parts = lax.axis_size("coef")
    rows = switch_ref.shape[1]

    def member(step):
        y, x, z = STEPS[step]
        return (me_y + y) % 2 * 8 + (me_x + x) % 4 * 2 + (me_z + z) % 2

    barrier = pltpu.get_barrier_semaphore()
    for step in range(1, MEMBERS):
        pl.semaphore_signal(barrier, inc=1, device_id=(base + member(step), coef), device_id_type=MESH)
    other_core = coef + 1 - 2 * (coef % 2)
    pl.semaphore_signal(barrier, inc=1, device_id=(box, other_core), device_id_type=MESH)
    for step in range(2, parts, 2):
        pl.semaphore_signal(barrier, inc=1, device_id=(box, (coef + step) % parts), device_id_type=MESH)
    pl.semaphore_wait(barrier, MEMBERS - 1 + parts // 2)

    def window(j):
        return offsets_ref.at[:, pl.ds(pl.multiple_of(128 * (3 * (j // 2) + j % 2), 128), WINDOW)]

    def send(src, dst, send_sem, recv_sem, j):
        return pltpu.make_async_remote_copy(
            src, dst, send_sem, recv_sem, device_id=(base + j, coef), device_id_type=MESH
        )

    def at(c):
        return pl.ds(pl.multiple_of(c * CHUNK, CHUNK), CHUNK)

    def rows_of(owner):
        return whole.at[:, pl.ds(pl.multiple_of(owner * rows, rows), rows)]

    def piece(src, owner, recv_sem, target):
        return pltpu.make_async_remote_copy(
            src, rows_of(owner), sw_send, recv_sem, device_id=(box, target), device_id_type=MESH
        )

    for step in range(2, parts, 2):
        piece(switch_ref, coef, sw_recv, (coef + step) % parts).start()
    pltpu.make_async_copy(switch_ref, rows_of(coef), sw_recv).start()

    def send_in(c, carry):
        for step in range(1, MEMBERS):
            j = member(step)
            send(coef_ref.at[j, at(c)], arrived.at[me, at(c)], in_send, in_recv.at[c], j).start()
        pltpu.make_async_copy(coef_ref.at[me, at(c)], arrived.at[me, at(c)], in_recv.at[c]).start()
        return carry

    send_in(0, 0)
    for step in range(1, MEMBERS):
        j = member(step)
        send(window(j), windows.at[me], off_send, off_recv, j).start()
    pltpu.make_async_copy(window(me), windows.at[me], off_recv).start()
    lax.fori_loop(1, chunks, send_in, 0)

    loads = []
    for level in range(levels):
        for bit in range(2):
            for side in range(2):
                pair = interp_ref.at[level, bit, bit if side == 0 else 1 - bit]
                top = 2 * rank * side
                for part, row, column in ((0, 0, 0), (1, 0, rank), (0, rank, rank)):
                    loads.append(pltpu.make_async_copy(
                        pair.at[part],
                        weights.at[level, bit, pl.ds(top + row, rank), pl.ds(column, rank)],
                        weight_sem.at[len(loads)],
                    ))
    for load in loads:
        load.start()
    for load in loads:
        load.wait()

    def negate(i, carry):
        level, bit, side = i // 4, i // 2 % 2, i % 2
        top = 2 * rank * side
        weights[level, bit, pl.ds(pl.multiple_of(top + rank, rank), rank), :rank] = -weights[
            level, bit, pl.ds(pl.multiple_of(top, rank), rank), rank:
        ]
        return carry

    lax.fori_loop(0, 4 * levels, negate, 0)

    pltpu.make_async_copy(windows, windows, off_recv).wait()
    columns[...] = jnp.transpose(
        windows[...].reshape(2 * MEMBERS, WINDOW).astype(jnp.float32), (1, 0)
    )
    points = lax.broadcasted_iota(jnp.int32, (1, rank), 1)
    point_x = (points // SIDE).astype(jnp.float32)
    point_y = (points % SIDE).astype(jnp.float32)
    skip = 64 * (me % 2)

    def compute(c, carry):
        pair = columns[pl.ds(pl.multiple_of(skip + c * CHUNK, 32), CHUNK), :]
        for b in range(MEMBERS):
            phase = pair[:, 2 * b:2 * b + 1] * point_x + pair[:, 2 * b + 1:2 * b + 2] * point_y
            cosine, sine = turn(phase)
            cosines[b] = cosine
            sines[b] = sine

        pltpu.make_async_copy(arrived.at[:, at(c)], arrived.at[:, at(c)], in_recv.at[c]).wait()

        for b in range(MEMBERS):
            state = arrived[b, at(c), :].astype(jnp.float32)
            real, imag = state[:, :rank], state[:, rank:]
            cosine, sine = cosines[b], sines[b]
            rotated[0, b, :, :rank] = (real * cosine - imag * sine).astype(jnp.bfloat16)
            rotated[0, b, :, rank:] = (real * sine + imag * cosine).astype(jnp.bfloat16)

        for level in range(levels):
            now, later = level % 2, 1 - level % 2
            for bit in range(2):
                own = jnp.concatenate([rotated[now, b] for b in boxes_with(bit, level)], axis=0)
                cross = jnp.concatenate(
                    [rotated[now, b ^ 1 << level] for b in boxes_with(bit, level)], axis=0
                )
                state = jnp.dot(
                    jnp.concatenate([own, cross], axis=1), weights[level, bit],
                    preferred_element_type=jnp.float32,
                )
                for k, b in enumerate(boxes_with(bit, level)):
                    mine = state[k * CHUNK:(k + 1) * CHUNK]
                    if level == levels - 1:
                        leaving[b, at(c), :] = mine.astype(jnp.bfloat16)
                        continue
                    cosine, sine = cosines[b], sines[b]
                    before_c = cosine if level == 0 else cosine_now[b]
                    before_s = sine if level == 0 else sine_now[b]
                    next_c = before_c * cosine - before_s * sine
                    next_s = before_c * sine + before_s * cosine
                    if level < levels - 2:
                        cosine_now[b] = next_c
                        sine_now[b] = next_s
                    real, imag = mine[:, :rank], mine[:, rank:]
                    rotated[later, b, :, :rank] = (real * next_c - imag * next_s).astype(jnp.bfloat16)
                    rotated[later, b, :, rank:] = (real * next_s + imag * next_c).astype(jnp.bfloat16)

        for step in range(1, MEMBERS):
            j = member(step)
            send(leaving.at[j, at(c)], home.at[me, at(c)], out_send, out_recv.at[c], j).start()
        pltpu.make_async_copy(leaving.at[me, at(c)], home.at[me, at(c)], out_recv.at[c]).start()
        return carry

    lax.fori_loop(0, chunks, compute, 0)

    half = whole.at[:, pl.ds(0, rows * (parts // 2))]
    pltpu.make_async_copy(half, half, sw_recv).wait()
    for step in range(0, parts, 2):
        owner = (coef + step) % parts
        piece(rows_of(owner), owner, sw_other, other_core).start()
    pltpu.make_async_copy(half, half, sw_other).wait()
    matrix[:rank, :rank] = whole[0]
    matrix[:rank, rank:] = whole[1]
    matrix[rank:, :rank] = -whole[1]
    matrix[rank:, rank:] = whole[0]

    def finish(c, carry):
        pltpu.make_async_copy(home.at[:, at(c)], home.at[:, at(c)], out_recv.at[c]).wait()
        state = home[:, at(c), :].reshape(MEMBERS * CHUNK, 2 * rank)
        switched = jnp.dot(state, matrix[...], preferred_element_type=jnp.float32)
        early_ref[:, at(c), :] = switched.reshape(MEMBERS, CHUNK, 2 * rank)
        return carry

    lax.fori_loop(0, chunks - 1, finish, 0)
    latest = home.at[:, at(chunks - 1)]
    pltpu.make_async_copy(latest, latest, out_recv.at[chunks - 1]).wait()

    others = pl.ds(0, MEMBERS - 1)
    send(coef_ref.at[others], arrived.at[others], in_send, off_recv, member(1)).wait_send()
    send(leaving.at[others], home.at[others], out_send, off_recv, member(1)).wait_send()
    send(windows.at[others], windows.at[others], off_send, off_recv, member(1)).wait_send()
    sent = whole.at[:, pl.ds(0, rows * (parts - 1))]
    send(sent, sent, sw_send, off_recv, member(1)).wait_send()


def flush(early_ref, home_ref, matrix_ref, out_ref, late, early_sem, late_sem):
    done, width = early_ref.shape[1], matrix_ref.shape[-1]
    early = [
        pltpu.make_async_copy(
            early_ref.at[pl.ds(i, PIECE)], out_ref.at[pl.ds(i, PIECE), pl.ds(0, done)], early_sem.at[i // PIECE]
        )
        for i in range(0, MEMBERS, PIECE)
    ]
    for copy in early:
        copy.start()
    copies = []
    for i in range(0, MEMBERS, PIECE):
        state = home_ref[i:i + PIECE, done:, :].reshape(PIECE * CHUNK, width)
        switched = jnp.dot(state, matrix_ref[...], preferred_element_type=jnp.float32)
        late[i:i + PIECE] = switched.reshape(PIECE, CHUNK, width)
        copies.append(pltpu.make_async_copy(
            late.at[pl.ds(i, PIECE)], out_ref.at[pl.ds(i, PIECE), pl.ds(done, CHUNK)], late_sem.at[i // PIECE]
        ))
        copies[-1].start()
    for copy in early + copies:
        copy.wait()


def body(coefficients, interp, switch, grid_offsets):
    _, rows, width = coefficients.shape
    rank = interp.shape[-1]
    levels = interp.shape[0]
    share = rows // MEMBERS
    chunks = share // CHUNK
    bf16, f32 = jnp.bfloat16, jnp.float32
    dma = pltpu.SemaphoreType.DMA
    operands = (
        coefficients.reshape(MEMBERS, share, width), interp, switch[0], jnp.swapaxes(grid_offsets[0], 0, 1)
    )
    early, home, matrix = pl.pallas_call(
        middle,
        out_shape=(
            pltpu.VMEM((MEMBERS, share - CHUNK, width), f32),
            pltpu.VMEM((MEMBERS, share, width), bf16),
            pltpu.VMEM((width, width), bf16),
        ),
        in_specs=[pl.BlockSpec(memory_space=pl.ANY)] * 4,
        out_specs=(pl.BlockSpec(memory_space=pltpu.VMEM),) * 3,
        scratch_shapes=[
            pltpu.VMEM((MEMBERS, share, width), bf16),
            pltpu.VMEM((MEMBERS, share, width), bf16),
            pltpu.VMEM((levels, 2, 2 * width, width), bf16),
            pltpu.VMEM((2, rank, rank), bf16),
            pltpu.VMEM((MEMBERS, 2, WINDOW), jnp.int32),
            pltpu.VMEM((WINDOW, 2 * MEMBERS), f32),
            pltpu.VMEM((MEMBERS, CHUNK, rank), f32),
            pltpu.VMEM((MEMBERS, CHUNK, rank), f32),
            pltpu.VMEM((MEMBERS, CHUNK, rank), f32),
            pltpu.VMEM((MEMBERS, CHUNK, rank), f32),
            pltpu.VMEM((2, MEMBERS, CHUNK, width), bf16),
            dma, dma((chunks,)), dma, dma((chunks,)), dma, dma, dma, dma, dma, dma((12 * levels,)),
        ],
        compiler_params=pltpu.CompilerParams(
            collective_id=0, has_side_effects=True, vmem_limit_bytes=50 << 20
        ),
        name="middle",
    )(*[pltpu.with_memory_space_constraint(operand, pltpu.HBM) for operand in operands])
    switched = pl.pallas_call(
        flush,
        out_shape=jax.ShapeDtypeStruct((MEMBERS, share, width), f32),
        in_specs=[pl.BlockSpec(memory_space=pltpu.VMEM)] * 3,
        out_specs=pl.BlockSpec(memory_space=pl.ANY),
        scratch_shapes=[
            pltpu.VMEM((MEMBERS, CHUNK, width), f32), dma((MEMBERS // PIECE,)), dma((MEMBERS // PIECE,))
        ],
        compiler_params=pltpu.CompilerParams(vmem_limit_bytes=16 << 20),
        name="flush",
    )(*[pltpu.with_memory_space_constraint(operand, pltpu.VMEM) for operand in (early, home, matrix)])
    return switched.reshape(1, rows, width)


def solution(mesh):
    in_specs = (P("box", "coef", None), P(), P("box", None, "coef", None), P("box", "coef", None))
    out_specs = P("box", "coef", None)
    return jax.shard_map(body, mesh=mesh, in_specs=in_specs, out_specs=out_specs, check_vma=False)
```

```python
import math

import jax
import jax.numpy as jnp
from jax import lax
from jax.experimental import pallas as pl
from jax.experimental.pallas import tpu as pltpu
from jax.sharding import PartitionSpec as P

SIDE = 16
MEMBERS = 16
CHUNK = 96
PIECE = 2
WINDOW = 256
MESH = pl.DeviceIdType.MESH
STEPS = [(0, 0, 0)] + [
    (y, x, z) for x, y in ((0, 0), (1, 0), (2, 0), (3, 0), (0, 1), (1, 1), (2, 1), (3, 1)) for z in (1, 0) if x + y + z
]


def turn(phase):
    share = phase * (1.0 / 64.0)
    share = share - jnp.floor(share + 0.5)
    half = share * math.pi
    square = half * half
    sine = half * (1.0 + square * (-1.0 / 6 + square * (1.0 / 120 + square * (-1.0 / 5040 + square * (
        1.0 / 362880 + square * (-1.0 / 39916800 + square * (1.0 / 6227020800)))))))
    cosine = 1.0 + square * (-0.5 + square * (1.0 / 24 + square * (-1.0 / 720 + square * (
        1.0 / 40320 + square * (-1.0 / 3628800 + square * (1.0 / 479001600))))))
    return 1.0 - 2.0 * sine * sine, 2.0 * sine * cosine


def boxes_with(bit, level):
    return [b for b in range(MEMBERS) if b >> level & 1 == bit]


def middle(
    coef_ref, interp_ref, switch_ref, offsets_ref, home, matrix,
    arrived, leaving, weights, whole, windows, columns,
    cosines, sines, cosine_now, sine_now, rotated,
    in_send, in_recv, out_send, out_recv, off_send, off_recv, sw_send, sw_recv, sw_other, weight_sem,
):
    box, coef = lax.axis_index("box"), lax.axis_index("coef")
    me, base = box % MEMBERS, box // MEMBERS * MEMBERS
    me_y, me_x, me_z = me // 8, me // 2 % 4, me % 2
    share = coef_ref.shape[1]
    rank = interp_ref.shape[-1]
    levels = interp_ref.shape[0]
    chunks = share // CHUNK
    parts = lax.axis_size("coef")
    rows = switch_ref.shape[1]

    def member(step):
        y, x, z = STEPS[step]
        return (me_y + y) % 2 * 8 + (me_x + x) % 4 * 2 + (me_z + z) % 2

    barrier = pltpu.get_barrier_semaphore()
    for step in range(1, MEMBERS):
        pl.semaphore_signal(barrier, inc=1, device_id=(base + member(step), coef), device_id_type=MESH)
    other_core = coef + 1 - 2 * (coef % 2)
    pl.semaphore_signal(barrier, inc=1, device_id=(box, other_core), device_id_type=MESH)
    for step in range(2, parts, 2):
        pl.semaphore_signal(barrier, inc=1, device_id=(box, (coef + step) % parts), device_id_type=MESH)
    pl.semaphore_wait(barrier, MEMBERS - 1 + parts // 2)

    def window(j):
        return offsets_ref.at[:, pl.ds(pl.multiple_of(128 * (3 * (j // 2) + j % 2), 128), WINDOW)]

    def send(src, dst, send_sem, recv_sem, j):
        return pltpu.make_async_remote_copy(
            src, dst, send_sem, recv_sem, device_id=(base + j, coef), device_id_type=MESH
        )

    def at(c):
        return pl.ds(pl.multiple_of(c * CHUNK, CHUNK), CHUNK)

    def rows_of(owner):
        return whole.at[:, pl.ds(pl.multiple_of(owner * rows, rows), rows)]

    def piece(src, owner, recv_sem, target):
        return pltpu.make_async_remote_copy(
            src, rows_of(owner), sw_send, recv_sem, device_id=(box, target), device_id_type=MESH
        )

    for step in range(2, parts, 2):
        piece(switch_ref, coef, sw_recv, (coef + step) % parts).start()
    pltpu.make_async_copy(switch_ref, rows_of(coef), sw_recv).start()

    def send_in(c, carry):
        for step in range(1, MEMBERS):
            j = member(step)
            send(coef_ref.at[j, at(c)], arrived.at[me, at(c)], in_send, in_recv.at[c], j).start()
        pltpu.make_async_copy(coef_ref.at[me, at(c)], arrived.at[me, at(c)], in_recv.at[c]).start()
        return carry

    send_in(0, 0)
    for step in range(1, MEMBERS):
        j = member(step)
        send(window(j), windows.at[me], off_send, off_recv, j).start()
    pltpu.make_async_copy(window(me), windows.at[me], off_recv).start()
    lax.fori_loop(1, chunks, send_in, 0)

    loads = []
    for level in range(levels):
        for bit in range(2):
            for side in range(2):
                pair = interp_ref.at[level, bit, bit if side == 0 else 1 - bit]
                top = 2 * rank * side
                for part, row, column in ((0, 0, 0), (1, 0, rank), (0, rank, rank)):
                    loads.append(pltpu.make_async_copy(
                        pair.at[part],
                        weights.at[level, bit, pl.ds(top + row, rank), pl.ds(column, rank)],
                        weight_sem.at[len(loads)],
                    ))
    for load in loads:
        load.start()
    for load in loads:
        load.wait()

    def negate(i, carry):
        level, bit, side = i // 4, i // 2 % 2, i % 2
        top = 2 * rank * side
        weights[level, bit, pl.ds(pl.multiple_of(top + rank, rank), rank), :rank] = -weights[
            level, bit, pl.ds(pl.multiple_of(top, rank), rank), rank:
        ]
        return carry

    lax.fori_loop(0, 4 * levels, negate, 0)

    pltpu.make_async_copy(windows, windows, off_recv).wait()
    columns[...] = jnp.transpose(
        windows[...].reshape(2 * MEMBERS, WINDOW).astype(jnp.float32), (1, 0)
    )
    points = lax.broadcasted_iota(jnp.int32, (1, rank), 1)
    point_x = (points // SIDE).astype(jnp.float32)
    point_y = (points % SIDE).astype(jnp.float32)
    skip = 64 * (me % 2)

    def compute(c, carry):
        pair = columns[pl.ds(pl.multiple_of(skip + c * CHUNK, 32), CHUNK), :]
        for b in range(MEMBERS):
            phase = pair[:, 2 * b:2 * b + 1] * point_x + pair[:, 2 * b + 1:2 * b + 2] * point_y
            cosine, sine = turn(phase)
            cosines[b] = cosine
            sines[b] = sine

        pltpu.make_async_copy(arrived.at[:, at(c)], arrived.at[:, at(c)], in_recv.at[c]).wait()

        for b in range(MEMBERS):
            state = arrived[b, at(c), :].astype(jnp.float32)
            real, imag = state[:, :rank], state[:, rank:]
            cosine, sine = cosines[b], sines[b]
            rotated[0, b, :, :rank] = (real * cosine - imag * sine).astype(jnp.bfloat16)
            rotated[0, b, :, rank:] = (real * sine + imag * cosine).astype(jnp.bfloat16)

        for level in range(levels):
            now, later = level % 2, 1 - level % 2
            for bit in range(2):
                own = jnp.concatenate([rotated[now, b] for b in boxes_with(bit, level)], axis=0)
                cross = jnp.concatenate(
                    [rotated[now, b ^ 1 << level] for b in boxes_with(bit, level)], axis=0
                )
                state = jnp.dot(
                    jnp.concatenate([own, cross], axis=1), weights[level, bit],
                    preferred_element_type=jnp.float32,
                )
                for k, b in enumerate(boxes_with(bit, level)):
                    mine = state[k * CHUNK:(k + 1) * CHUNK]
                    if level == levels - 1:
                        leaving[b, at(c), :] = mine.astype(jnp.bfloat16)
                        continue
                    cosine, sine = cosines[b], sines[b]
                    before_c = cosine if level == 0 else cosine_now[b]
                    before_s = sine if level == 0 else sine_now[b]
                    next_c = before_c * cosine - before_s * sine
                    next_s = before_c * sine + before_s * cosine
                    if level < levels - 2:
                        cosine_now[b] = next_c
                        sine_now[b] = next_s
                    real, imag = mine[:, :rank], mine[:, rank:]
                    rotated[later, b, :, :rank] = (real * next_c - imag * next_s).astype(jnp.bfloat16)
                    rotated[later, b, :, rank:] = (real * next_s + imag * next_c).astype(jnp.bfloat16)

        for step in range(1, MEMBERS):
            j = member(step)
            send(leaving.at[j, at(c)], home.at[me, at(c)], out_send, out_recv.at[c], j).start()
        pltpu.make_async_copy(leaving.at[me, at(c)], home.at[me, at(c)], out_recv.at[c]).start()
        return carry

    lax.fori_loop(0, chunks, compute, 0)

    half = whole.at[:, pl.ds(0, rows * (parts // 2))]
    pltpu.make_async_copy(half, half, sw_recv).wait()
    for step in range(0, parts, 2):
        owner = (coef + step) % parts
        piece(rows_of(owner), owner, sw_other, other_core).start()
    pltpu.make_async_copy(half, half, sw_other).wait()
    matrix[:rank, :rank] = whole[0]
    matrix[:rank, rank:] = whole[1]
    matrix[rank:, :rank] = -whole[1]
    matrix[rank:, rank:] = whole[0]

    for c in range(chunks):
        pltpu.make_async_copy(home.at[:, at(c)], home.at[:, at(c)], out_recv.at[c]).wait()

    others = pl.ds(0, MEMBERS - 1)
    send(coef_ref.at[others], arrived.at[others], in_send, off_recv, member(1)).wait_send()
    send(leaving.at[others], home.at[others], out_send, off_recv, member(1)).wait_send()
    send(windows.at[others], windows.at[others], off_send, off_recv, member(1)).wait_send()
    sent = whole.at[:, pl.ds(0, rows * (parts - 1))]
    send(sent, sent, sw_send, off_recv, member(1)).wait_send()


def flush(home_ref, matrix_ref, out_ref, result, sems):
    _, share, width = home_ref.shape
    copies = []
    for i in range(0, MEMBERS, PIECE):
        state = home_ref[i:i + PIECE].reshape(PIECE * share, width)
        switched = jnp.dot(state, matrix_ref[...], preferred_element_type=jnp.float32)
        result[i:i + PIECE] = switched.reshape(PIECE, share, width)
        copies.append(pltpu.make_async_copy(
            result.at[pl.ds(i, PIECE)], out_ref.at[pl.ds(i, PIECE)], sems.at[i // PIECE]
        ))
        copies[-1].start()
    for copy in copies:
        copy.wait()


def body(coefficients, interp, switch, grid_offsets):
    _, rows, width = coefficients.shape
    rank = interp.shape[-1]
    levels = interp.shape[0]
    share = rows // MEMBERS
    chunks = share // CHUNK
    bf16, f32 = jnp.bfloat16, jnp.float32
    dma = pltpu.SemaphoreType.DMA
    operands = (
        coefficients.reshape(MEMBERS, share, width), interp, switch[0], jnp.swapaxes(grid_offsets[0], 0, 1)
    )
    home, matrix = pl.pallas_call(
        middle,
        out_shape=(
            pltpu.VMEM((MEMBERS, share, width), bf16),
            pltpu.VMEM((width, width), bf16),
        ),
        in_specs=[pl.BlockSpec(memory_space=pl.ANY)] * 4,
        out_specs=(pl.BlockSpec(memory_space=pltpu.VMEM),) * 2,
        scratch_shapes=[
            pltpu.VMEM((MEMBERS, share, width), bf16),
            pltpu.VMEM((MEMBERS, share, width), bf16),
            pltpu.VMEM((levels, 2, 2 * width, width), bf16),
            pltpu.VMEM((2, rank, rank), bf16),
            pltpu.VMEM((MEMBERS, 2, WINDOW), jnp.int32),
            pltpu.VMEM((WINDOW, 2 * MEMBERS), f32),
            pltpu.VMEM((MEMBERS, CHUNK, rank), f32),
            pltpu.VMEM((MEMBERS, CHUNK, rank), f32),
            pltpu.VMEM((MEMBERS, CHUNK, rank), f32),
            pltpu.VMEM((MEMBERS, CHUNK, rank), f32),
            pltpu.VMEM((2, MEMBERS, CHUNK, width), bf16),
            dma, dma((chunks,)), dma, dma((chunks,)), dma, dma, dma, dma, dma, dma((12 * levels,)),
        ],
        compiler_params=pltpu.CompilerParams(
            collective_id=0, has_side_effects=True, vmem_limit_bytes=50 << 20
        ),
        name="middle",
    )(*[pltpu.with_memory_space_constraint(operand, pltpu.HBM) for operand in operands])
    switched = pl.pallas_call(
        flush,
        out_shape=jax.ShapeDtypeStruct((MEMBERS, share, width), f32),
        in_specs=[pl.BlockSpec(memory_space=pltpu.VMEM)] * 2,
        out_specs=pl.BlockSpec(memory_space=pl.ANY),
        scratch_shapes=[
            pltpu.VMEM((MEMBERS, share, width), f32), dma((MEMBERS // PIECE,))
        ],
        compiler_params=pltpu.CompilerParams(vmem_limit_bytes=16 << 20),
        name="flush",
    )(*[pltpu.with_memory_space_constraint(operand, pltpu.VMEM) for operand in (home, matrix)])
    return switched.reshape(1, rows, width)


def solution(mesh):
    in_specs = (P("box", "coef", None), P(), P("box", None, "coef", None), P("box", "coef", None))
    out_specs = P("box", "coef", None)
    return jax.shard_map(body, mesh=mesh, in_specs=in_specs, out_specs=out_specs, check_vma=False)
```

```python
import math

import jax
import jax.numpy as jnp
from jax import lax
from jax.experimental import pallas as pl
from jax.experimental.pallas import tpu as pltpu
from jax.sharding import PartitionSpec as P

SIDE = 16
MEMBERS = 16
CHUNK = 96
PIECE = 2
WINDOW = 256
MESH = pl.DeviceIdType.MESH
STEPS = [(0, 0, 0)] + [
    (y, x, z) for x, y in ((2, 1), (1, 1), (3, 1), (2, 0), (1, 0), (3, 0), (0, 1), (0, 0)) for z in (1, 0) if x + y + z
]


def turn(phase):
    share = phase * (1.0 / 64.0)
    share = share - jnp.floor(share + 0.5)
    half = share * math.pi
    square = half * half
    sine = half * (1.0 + square * (-1.0 / 6 + square * (1.0 / 120 + square * (-1.0 / 5040 + square * (
        1.0 / 362880 + square * (-1.0 / 39916800 + square * (1.0 / 6227020800)))))))
    cosine = 1.0 + square * (-0.5 + square * (1.0 / 24 + square * (-1.0 / 720 + square * (
        1.0 / 40320 + square * (-1.0 / 3628800 + square * (1.0 / 479001600))))))
    return 1.0 - 2.0 * sine * sine, 2.0 * sine * cosine


def boxes_with(bit, level):
    return [b for b in range(MEMBERS) if b >> level & 1 == bit]


def middle(
    coef_ref, interp_ref, switch_ref, offsets_ref, home, matrix,
    arrived, leaving, weights, whole, windows, columns,
    cosines, sines, cosine_now, sine_now, rotated,
    in_send, in_recv, out_send, out_recv, off_send, off_recv, sw_send, sw_recv, sw_other, weight_sem,
):
    box, coef = lax.axis_index("box"), lax.axis_index("coef")
    me, base = box % MEMBERS, box // MEMBERS * MEMBERS
    me_y, me_x, me_z = me // 8, me // 2 % 4, me % 2
    share = coef_ref.shape[1]
    rank = interp_ref.shape[-1]
    levels = interp_ref.shape[0]
    chunks = share // CHUNK
    parts = lax.axis_size("coef")
    rows = switch_ref.shape[1]

    def member(step):
        y, x, z = STEPS[step]
        return (me_y + y) % 2 * 8 + (me_x + x) % 4 * 2 + (me_z + z) % 2

    barrier = pltpu.get_barrier_semaphore()
    for step in range(1, MEMBERS):
        pl.semaphore_signal(barrier, inc=1, device_id=(base + member(step), coef), device_id_type=MESH)
    other_core = coef + 1 - 2 * (coef % 2)
    pl.semaphore_signal(barrier, inc=1, device_id=(box, other_core), device_id_type=MESH)
    for step in range(2, parts, 2):
        pl.semaphore_signal(barrier, inc=1, device_id=(box, (coef + step) % parts), device_id_type=MESH)
    pl.semaphore_wait(barrier, MEMBERS - 1 + parts // 2)

    def window(j):
        return offsets_ref.at[:, pl.ds(pl.multiple_of(128 * (3 * (j // 2) + j % 2), 128), WINDOW)]

    def send(src, dst, send_sem, recv_sem, j):
        return pltpu.make_async_remote_copy(
            src, dst, send_sem, recv_sem, device_id=(base + j, coef), device_id_type=MESH
        )

    def at(c):
        return pl.ds(pl.multiple_of(c * CHUNK, CHUNK), CHUNK)

    def rows_of(owner):
        return whole.at[:, pl.ds(pl.multiple_of(owner * rows, rows), rows)]

    def piece(src, owner, recv_sem, target):
        return pltpu.make_async_remote_copy(
            src, rows_of(owner), sw_send, recv_sem, device_id=(box, target), device_id_type=MESH
        )

    for step in range(2, parts, 2):
        piece(switch_ref, coef, sw_recv, (coef + step) % parts).start()
    pltpu.make_async_copy(switch_ref, rows_of(coef), sw_recv).start()

    def send_in(c, carry):
        for step in range(1, MEMBERS):
            j = member(step)
            send(coef_ref.at[j, at(c)], arrived.at[me, at(c)], in_send, in_recv.at[c], j).start()
        pltpu.make_async_copy(coef_ref.at[me, at(c)], arrived.at[me, at(c)], in_recv.at[c]).start()
        return carry

    send_in(0, 0)
    for step in range(1, MEMBERS):
        j = member(step)
        send(window(j), windows.at[me], off_send, off_recv, j).start()
    pltpu.make_async_copy(window(me), windows.at[me], off_recv).start()
    lax.fori_loop(1, chunks, send_in, 0)

    loads = []
    for level in range(levels):
        for bit in range(2):
            for side in range(2):
                pair = interp_ref.at[level, bit, bit if side == 0 else 1 - bit]
                top = 2 * rank * side
                for part, row, column in ((0, 0, 0), (1, 0, rank), (0, rank, rank)):
                    loads.append(pltpu.make_async_copy(
                        pair.at[part],
                        weights.at[level, bit, pl.ds(top + row, rank), pl.ds(column, rank)],
                        weight_sem.at[len(loads)],
                    ))
    for load in loads:
        load.start()
    for load in loads:
        load.wait()

    def negate(i, carry):
        level, bit, side = i // 4, i // 2 % 2, i % 2
        top = 2 * rank * side
        weights[level, bit, pl.ds(pl.multiple_of(top + rank, rank), rank), :rank] = -weights[
            level, bit, pl.ds(pl.multiple_of(top, rank), rank), rank:
        ]
        return carry

    lax.fori_loop(0, 4 * levels, negate, 0)

    pltpu.make_async_copy(windows, windows, off_recv).wait()
    columns[...] = jnp.transpose(
        windows[...].reshape(2 * MEMBERS, WINDOW).astype(jnp.float32), (1, 0)
    )
    points = lax.broadcasted_iota(jnp.int32, (1, rank), 1)
    point_x = (points // SIDE).astype(jnp.float32)
    point_y = (points % SIDE).astype(jnp.float32)
    skip = 64 * (me % 2)

    def compute(c, carry):
        pair = columns[pl.ds(pl.multiple_of(skip + c * CHUNK, 32), CHUNK), :]
        for b in range(MEMBERS):
            phase = pair[:, 2 * b:2 * b + 1] * point_x + pair[:, 2 * b + 1:2 * b + 2] * point_y
            cosine, sine = turn(phase)
            cosines[b] = cosine
            sines[b] = sine

        pltpu.make_async_copy(arrived.at[:, at(c)], arrived.at[:, at(c)], in_recv.at[c]).wait()

        for b in range(MEMBERS):
            state = arrived[b, at(c), :].astype(jnp.float32)
            real, imag = state[:, :rank], state[:, rank:]
            cosine, sine = cosines[b], sines[b]
            rotated[0, b, :, :rank] = (real * cosine - imag * sine).astype(jnp.bfloat16)
            rotated[0, b, :, rank:] = (real * sine + imag * cosine).astype(jnp.bfloat16)

        for level in range(levels):
            now, later = level % 2, 1 - level % 2
            for bit in range(2):
                own = jnp.concatenate([rotated[now, b] for b in boxes_with(bit, level)], axis=0)
                cross = jnp.concatenate(
                    [rotated[now, b ^ 1 << level] for b in boxes_with(bit, level)], axis=0
                )
                state = jnp.dot(
                    jnp.concatenate([own, cross], axis=1), weights[level, bit],
                    preferred_element_type=jnp.float32,
                )
                for k, b in enumerate(boxes_with(bit, level)):
                    mine = state[k * CHUNK:(k + 1) * CHUNK]
                    if level == levels - 1:
                        leaving[b, at(c), :] = mine.astype(jnp.bfloat16)
                        continue
                    cosine, sine = cosines[b], sines[b]
                    before_c = cosine if level == 0 else cosine_now[b]
                    before_s = sine if level == 0 else sine_now[b]
                    next_c = before_c * cosine - before_s * sine
                    next_s = before_c * sine + before_s * cosine
                    if level < levels - 2:
                        cosine_now[b] = next_c
                        sine_now[b] = next_s
                    real, imag = mine[:, :rank], mine[:, rank:]
                    rotated[later, b, :, :rank] = (real * next_c - imag * next_s).astype(jnp.bfloat16)
                    rotated[later, b, :, rank:] = (real * next_s + imag * next_c).astype(jnp.bfloat16)

        for step in range(1, MEMBERS):
            j = member(step)
            send(leaving.at[j, at(c)], home.at[me, at(c)], out_send, out_recv.at[c], j).start()
        pltpu.make_async_copy(leaving.at[me, at(c)], home.at[me, at(c)], out_recv.at[c]).start()
        return carry

    lax.fori_loop(0, chunks, compute, 0)

    half = whole.at[:, pl.ds(0, rows * (parts // 2))]
    pltpu.make_async_copy(half, half, sw_recv).wait()
    for step in range(0, parts, 2):
        owner = (coef + step) % parts
        piece(rows_of(owner), owner, sw_other, other_core).start()
    pltpu.make_async_copy(half, half, sw_other).wait()
    matrix[:rank, :rank] = whole[0]
    matrix[:rank, rank:] = whole[1]
    matrix[rank:, :rank] = -whole[1]
    matrix[rank:, rank:] = whole[0]

    for c in range(chunks):
        pltpu.make_async_copy(home.at[:, at(c)], home.at[:, at(c)], out_recv.at[c]).wait()

    others = pl.ds(0, MEMBERS - 1)
    send(coef_ref.at[others], arrived.at[others], in_send, off_recv, member(1)).wait_send()
    send(leaving.at[others], home.at[others], out_send, off_recv, member(1)).wait_send()
    send(windows.at[others], windows.at[others], off_send, off_recv, member(1)).wait_send()
    sent = whole.at[:, pl.ds(0, rows * (parts - 1))]
    send(sent, sent, sw_send, off_recv, member(1)).wait_send()


def flush(home_ref, matrix_ref, out_ref, result, sems):
    _, share, width = home_ref.shape
    copies = []
    for i in range(0, MEMBERS, PIECE):
        state = home_ref[i:i + PIECE].reshape(PIECE * share, width)
        switched = jnp.dot(state, matrix_ref[...], preferred_element_type=jnp.float32)
        result[i:i + PIECE] = switched.reshape(PIECE, share, width)
        copies.append(pltpu.make_async_copy(
            result.at[pl.ds(i, PIECE)], out_ref.at[pl.ds(i, PIECE)], sems.at[i // PIECE]
        ))
        copies[-1].start()
    for copy in copies:
        copy.wait()


def body(coefficients, interp, switch, grid_offsets):
    _, rows, width = coefficients.shape
    rank = interp.shape[-1]
    levels = interp.shape[0]
    share = rows // MEMBERS
    chunks = share // CHUNK
    bf16, f32 = jnp.bfloat16, jnp.float32
    dma = pltpu.SemaphoreType.DMA
    operands = (
        coefficients.reshape(MEMBERS, share, width), interp, switch[0], jnp.swapaxes(grid_offsets[0], 0, 1)
    )
    home, matrix = pl.pallas_call(
        middle,
        out_shape=(
            pltpu.VMEM((MEMBERS, share, width), bf16),
            pltpu.VMEM((width, width), bf16),
        ),
        in_specs=[pl.BlockSpec(memory_space=pl.ANY)] * 4,
        out_specs=(pl.BlockSpec(memory_space=pltpu.VMEM),) * 2,
        scratch_shapes=[
            pltpu.VMEM((MEMBERS, share, width), bf16),
            pltpu.VMEM((MEMBERS, share, width), bf16),
            pltpu.VMEM((levels, 2, 2 * width, width), bf16),
            pltpu.VMEM((2, rank, rank), bf16),
            pltpu.VMEM((MEMBERS, 2, WINDOW), jnp.int32),
            pltpu.VMEM((WINDOW, 2 * MEMBERS), f32),
            pltpu.VMEM((MEMBERS, CHUNK, rank), f32),
            pltpu.VMEM((MEMBERS, CHUNK, rank), f32),
            pltpu.VMEM((MEMBERS, CHUNK, rank), f32),
            pltpu.VMEM((MEMBERS, CHUNK, rank), f32),
            pltpu.VMEM((2, MEMBERS, CHUNK, width), bf16),
            dma, dma((chunks,)), dma, dma((chunks,)), dma, dma, dma, dma, dma, dma((12 * levels,)),
        ],
        compiler_params=pltpu.CompilerParams(
            collective_id=0, has_side_effects=True, vmem_limit_bytes=50 << 20
        ),
        name="middle",
    )(*[pltpu.with_memory_space_constraint(operand, pltpu.HBM) for operand in operands])
    switched = pl.pallas_call(
        flush,
        out_shape=jax.ShapeDtypeStruct((MEMBERS, share, width), f32),
        in_specs=[pl.BlockSpec(memory_space=pltpu.VMEM)] * 2,
        out_specs=pl.BlockSpec(memory_space=pl.ANY),
        scratch_shapes=[
            pltpu.VMEM((MEMBERS, share, width), f32), dma((MEMBERS // PIECE,))
        ],
        compiler_params=pltpu.CompilerParams(vmem_limit_bytes=16 << 20),
        name="flush",
    )(*[pltpu.with_memory_space_constraint(operand, pltpu.VMEM) for operand in (home, matrix)])
    return switched.reshape(1, rows, width)


def solution(mesh):
    in_specs = (P("box", "coef", None), P(), P("box", None, "coef", None), P("box", "coef", None))
    out_specs = P("box", "coef", None)
    return jax.shard_map(body, mesh=mesh, in_specs=in_specs, out_specs=out_specs, check_vma=False)
```
